1024 devices in a mesh: energy: 32 (over y_lo, x, core), space: 32 (over z, y_hi).
Axes of the slice: x: 8, y: 8 (y_hi: 4, y_lo: 2; y = y_hi * 2 + y_lo), z: 8, core: 2. Of those that a mesh axis runs over, the one named last changes fastest.
Arguments:
- green: bfloat16 [4, 32, 32, 384, 384], P(None, 'energy', 'space'), may hold values from -6 to 6
- v_diag: bfloat16 [32, 384, 384], P('space'), may hold values from -0.3125 to 0.3125
- v_low: bfloat16 [32, 384, 384], P('space'), may hold values from -0.3125 to 0.3125
- energy_slot: int32 [32], replicated, may hold values from 0 to 31, each once
Outputs:
- sigma: bfloat16 [2, 32, 32, 384, 384], P(None, None, 'space', 'energy')
The draws below stay inside these ranges and needn't reach their ends.
Inputs may be any that keep to these rules, and one draw needn't show every extreme that they name: `energy_slot`: each grid energy appears in exactly one slot.
All inputs are finite; a program needn't handle non-finite values.
Results may differ from the reference program's by a relative error of at most 0.0066.
Values may be sent and summed in bfloat16 or wider, within the bound.
A program may use at most 32 MiB of HBM per device.

```python
import jax
import jax.numpy as jnp
from jax import lax

B = 384
NE = 32
NB = 32


def level_of(own_key, shape, cuts, low, largest):
    def one(position, shards_of):
        steps = jax.random.uniform(jax.random.fold_in(jax.random.fold_in(own_key, 6), position), (shards_of,), jnp.float32, low / len(cuts), largest / len(cuts))
        return jnp.repeat(jnp.exp(steps), shape[position] // shards_of).reshape((-1,) + (1,) * (len(shape) - position - 1))

    factor_of = one(*cuts[0])
    for cut in cuts[1:]:
        factor_of = factor_of * one(*cut)
    return factor_of


def scatter_about(stream_key, shape, deviation, bound, split=(), kind=jnp.bfloat16):
    gain = level_of(stream_key, shape, split, -0.22, 0.18) if split else 1.0
    values = jax.random.normal(stream_key, shape, jnp.float32) * deviation * gain
    return jnp.minimum(jnp.maximum(values, -bound), bound).astype(kind)


def setup_inputs(seed: int = 0) -> dict:
    seeds = jax.random.split(jax.random.key(seed), 5)
    green = scatter_about(seeds[0], (4, NE, NB, B, B), 1.0, 6.0, ((1, 32), (2, 32)))
    v_diag = scatter_about(seeds[1], (NB, B, B), B ** -0.5, 0.3125, ((0, 32),))
    v_low = scatter_about(seeds[2], (NB, B, B), B ** -0.5, 0.3125, ((0, 32),))
    energy_slot = jax.random.permutation(seeds[3], NE).astype(jnp.int32)
    return {"green": green, "v_diag": v_diag, "v_low": v_low, "energy_slot": energy_slot}


def correlate_polar(grid):
    count = grid.shape[1]
    lesser = grid[0:2]
    greater = grid[2:4]
    padded = jnp.concatenate([lesser, jnp.zeros_like(lesser)], axis=1)

    def advance(offset, result):
        moved = lax.dynamic_slice_in_dim(padded, offset, count, 1)
        real_part = jnp.sum(moved[1] * greater[0] - moved[0] * greater[1], axis=0)
        imag_part = -jnp.sum(moved[0] * greater[0] + moved[1] * greater[1], axis=0)
        value = jnp.stack([real_part, imag_part])[:, None]
        return lax.dynamic_update_slice_in_dim(result, value, offset, 1)

    result = lax.fori_loop(0, count, advance, jnp.zeros_like(lesser))
    return result * (count ** -0.5)


def correlate_sigma(lesser, screened):
    count = lesser.shape[1]
    padded = jnp.concatenate([jnp.zeros_like(lesser), lesser], axis=1)

    def advance(offset, total):
        moved = lax.dynamic_slice_in_dim(padded, count - offset, count, 1)
        w_real = lax.dynamic_index_in_dim(screened[0], offset, 0, keepdims=True)
        w_imag = lax.dynamic_index_in_dim(screened[1], offset, 0, keepdims=True)
        real_part = -(moved[0] * w_imag + moved[1] * w_real)
        imag_part = moved[0] * w_real - moved[1] * w_imag
        return total + jnp.stack([real_part, imag_part])

    total = lax.fori_loop(0, count, advance, jnp.zeros_like(lesser))
    return total * (count ** -0.5)


def sandwich(matrix, polar):
    left = jnp.einsum("ij,cejk->ceik", matrix.astype(jnp.float32), polar.astype(jnp.float32)).astype(jnp.bfloat16)
    return jnp.einsum("ceij,kj->ceik", left.astype(jnp.float32), matrix.astype(jnp.float32))


def sandwich_t(matrix, polar):
    left = jnp.einsum("ji,cejk->ceik", matrix.astype(jnp.float32), polar.astype(jnp.float32)).astype(jnp.bfloat16)
    return jnp.einsum("ceij,jk->ceik", left.astype(jnp.float32), matrix.astype(jnp.float32))


def reference(green, v_diag, v_low, energy_slot):
    count = green.shape[1]
    blocks = green.shape[2]
    inverse = jnp.zeros((count,), jnp.int32).at[energy_slot].set(jnp.arange(count, dtype=jnp.int32))
    indices = jnp.arange(blocks, dtype=jnp.int32)

    def polar_block(index):
        block = green[:, :, index].astype(jnp.float32)[:, inverse]
        return correlate_polar(block).astype(jnp.bfloat16)[:, energy_slot]

    polar = lax.map(polar_block, indices)
    zero = jnp.zeros_like(polar[0])

    def sigma_block(index):
        own_polar = polar[index]
        below = jnp.where(index > 0, polar[jnp.maximum(index - 1, 0)], zero)
        above = jnp.where(index < blocks - 1, polar[jnp.minimum(index + 1, blocks - 1)], zero)
        coupling_up = v_low[jnp.minimum(index + 1, blocks - 1)]
        upper = lax.optimization_barrier(sandwich_t(coupling_up, above).astype(jnp.bfloat16)).astype(jnp.float32)
        total = sandwich(v_diag[index], own_polar) + sandwich(v_low[index], below) + upper
        screened = total.astype(jnp.bfloat16)[:, inverse].astype(jnp.float32)
        lesser = green[0:2, :, index].astype(jnp.float32)[:, inverse]
        return correlate_sigma(lesser, screened).astype(jnp.bfloat16)[:, energy_slot]

    sigma = lax.map(sigma_block, indices)
    return jnp.moveaxis(sigma, 0, 2)
```

```python
import functools

import jax
import jax.numpy as jnp
from jax import lax
from jax.experimental import pallas as pl
from jax.experimental.pallas import tpu as pltpu
from jax.sharding import PartitionSpec as P

F32 = jnp.float32
BF16 = jnp.bfloat16
MESH = pl.DeviceIdType.MESH
BLK = 8


def pack_green(green, chunks):
    _, size, _ = green.shape
    owners, width = size // 12, size // chunks
    g = green.reshape(2, 2, owners, 12, chunks, width).transpose(4, 2, 0, 1, 3, 5)
    top = g[:, :, :, :, :8].reshape(chunks, owners, 2, 16, width)
    low = g[:, :, :, :, 8:].reshape(chunks, owners, 2, 8, width)
    return jnp.concatenate([top, low], axis=3).reshape(chunks, owners, 48, width)


def group_index(position):
    owner = (position * 2731) >> 16
    inner = position - 24 * owner
    component = jnp.where(inner < 16, inner >> 3, (inner - 16) >> 2)
    row = jnp.where(inner < 16, inner & 7, 8 + (inner & 3))
    return component, 12 * owner + row


def dot(a, b, dims):
    return lax.dot_general(a, b, (dims, ((), ())), preferred_element_type=F32)


def kernel(ne, nb, chunks, slot_ref, green_ref, vd_ref, vl_ref, out_ref, *scratch):
    arr = scratch[0:chunks]
    abuf = scratch[chunks : 2 * chunks]
    warr = scratch[2 * chunks : 3 * chunks]
    (pout, wout, own, below, above, vup, fl, fg, grid_out, inv, spread, big_d, big_l, big_u,
     vl_own, vu_own, wacc, uacc, send_sem, recv_sem, space_send, space_recv) = scratch[3 * chunks :]
    size = vd_ref.shape[0]
    width = size // chunks
    me = lax.axis_index("energy")
    here = lax.axis_index("space")
    up = lax.rem(here + 1, nb)
    down = lax.rem(here + nb - 1, nb)
    scale = ne ** -0.5

    barrier = pltpu.get_barrier_semaphore()

    def greet(step, carry):
        peer = lax.rem(me + step, ne)
        pl.semaphore_signal(barrier, inc=1, device_id={"energy": peer, "space": here}, device_id_type=MESH)
        return carry

    lax.fori_loop(1, ne, greet, 0)
    for other in (up, down):
        pl.semaphore_signal(barrier, inc=1, device_id={"energy": me, "space": other}, device_id_type=MESH)
    pl.semaphore_wait(barrier, ne + 1)

    def to_space(src, dst, number, other):
        return pltpu.make_async_remote_copy(
            src_ref=src, dst_ref=dst, send_sem=space_send.at[number], recv_sem=space_recv.at[number],
            device_id={"energy": me, "space": other}, device_id_type=MESH)

    def exchange(phase, chunk, src, dst):
        number = phase * chunks + chunk

        def send(step, carry):
            peer = lax.rem(me + step, ne)
            pltpu.make_async_remote_copy(
                src_ref=src.at[peer], dst_ref=dst.at[me], send_sem=send_sem.at[number],
                recv_sem=recv_sem.at[number], device_id={"energy": peer, "space": here},
                device_id_type=MESH).start()
            return carry

        lax.fori_loop(1, ne, send, 0)
        pltpu.make_async_copy(src.at[me], dst.at[me], recv_sem.at[number]).start()

    def arrived(phase, chunk, dst):
        pltpu.make_async_copy(dst, dst, recv_sem.at[phase * chunks + chunk]).wait()

    def sent(phase, chunk, src):
        part = src.at[pl.ds(0, ne - 1)]
        pltpu.make_async_copy(part, part, send_sem.at[phase * chunks + chunk]).wait()

    for chunk in range(chunks):
        exchange(0, chunk, green_ref.at[chunk], arr[chunk])
    coupling = to_space(vl_ref, vup, 0, down)
    coupling.start()

    def invert(energy, carry):
        def look(slot, found):
            return jnp.where(slot_ref[slot] == energy, slot, found)

        inv[energy] = lax.fori_loop(0, ne, look, 0)
        return carry

    lax.fori_loop(0, ne, invert, 0)

    rows = 24 * ne
    _, row_of = group_index(lax.broadcasted_iota(jnp.int32, (rows, size), 0))
    spread[...] = jnp.where(row_of == lax.broadcasted_iota(jnp.int32, (rows, size), 1), 1.0, 0.0).astype(BF16)
    comp_a, _ = group_index(lax.broadcasted_iota(jnp.int32, (rows, rows), 0))
    comp_b, _ = group_index(lax.broadcasted_iota(jnp.int32, (rows, rows), 1))
    same = comp_a == comp_b

    def expand(matrix, dims):
        half = dot(spread[...], matrix, dims).astype(BF16)
        return jnp.where(same, dot(half, spread[...], ((1,), (1,))), 0.0).astype(BF16)

    big_d[...] = expand(vd_ref[...], ((1,), (0,)))
    vl_own[...] = jnp.where(here > 0, vl_ref[...], jnp.zeros_like(vl_ref))
    big_l[...] = expand(vl_own[...], ((1,), (0,)))

    zeros = jnp.zeros((BLK, 24, width), F32)
    for chunk in range(chunks):
        fl[chunk, 0:BLK] = zeros
        fl[chunk, BLK + ne : 2 * BLK + ne] = zeros
    top_rows = lax.broadcasted_iota(jnp.int32, (BLK, 8, width), 1) < 4

    def put_second(energy, value):
        fg[energy, 0:24] = value
        fg[energy, 24:32] = pltpu.roll(value[16:24], 4, 0)

    def products(window, energy, acc):
        a, b, m1, m2 = acc
        xr, xi, xm = window[:, 0:8], window[:, 8:16], window[:, 16:24]
        second = fg[energy]
        yr, yi, ym, ys = (second[8 * i : 8 * i + 8][None] for i in range(4))
        return xr, xi, yr, yi, a, b, m1 + xm * ym, m2 + xm * ys

    blank = tuple(jnp.zeros((BLK, 8, width), F32) for _ in range(4))

    def polar(chunk):
        arrived(0, chunk, arr[chunk])

        def place(energy, carry):
            value = arr[chunk][inv[energy]].astype(F32)
            fl[chunk, BLK + energy] = value[0:24]
            put_second(energy, value[24:48])
            return carry

        lax.fori_loop(0, ne, place, 0, unroll=4)
        for first in range(0, ne, BLK):
            def step(energy, acc):
                window = fl[chunk, pl.ds(BLK + first + energy, BLK)]
                xr, xi, yr, yi, a, b, m1, m2 = products(window, energy, acc)
                return a + (xi * yr - xr * yi), b + (xr * yr + xi * yi), m1, m2

            a, b, m1, m2 = lax.fori_loop(0, ne - first, step, blank, unroll=4)
            mixed = jnp.where(top_rows, pltpu.roll(m2, 4, 1) - m2, -(m1 + pltpu.roll(m1, 4, 1)))
            grid_out[first : first + BLK] = jnp.concatenate([a, -b, mixed], axis=1) * scale

        def to_slot(slot, carry):
            pout[chunk, slot] = grid_out[slot_ref[slot]].astype(BF16)
            return carry

        lax.fori_loop(0, ne, to_slot, 0, unroll=4)
        exchange(1, chunk, pout.at[chunk], abuf[chunk])

    for chunk in range(chunks):
        polar(chunk)

    coupling.wait()
    vu_own[...] = jnp.where(here < nb - 1, vup[...], jnp.zeros_like(vup))
    big_u[...] = expand(vu_own[...], ((1,), (1,)))

    copies = []
    for chunk in range(chunks):
        cols = slice(chunk * width, (chunk + 1) * width)
        arrived(1, chunk, abuf[chunk])
        own[chunk] = abuf[chunk][...].astype(F32).reshape(rows, width).astype(BF16)
        for number, dst, other in ((1 + chunk, below, up), (1 + chunks + chunk, above, down)):
            copy = to_space(own.at[chunk], dst.at[chunk], number, other)
            copy.start()
            copies.append(copy)
        left = dot(big_d[...], own[chunk], ((1,), (0,))).astype(BF16)
        part = dot(left, vd_ref[:, cols], ((1,), (1,)))
        wacc[...] = part if chunk == 0 else wacc[...] + part

    for chunk in range(chunks):
        cols = slice(chunk * width, (chunk + 1) * width)
        copies[2 * chunk].wait_recv()
        left = dot(big_l[...], below[chunk], ((1,), (0,))).astype(BF16)
        wacc[...] += dot(left, vl_own[:, cols], ((1,), (1,)))
        copies[2 * chunk + 1].wait_recv()
        left = dot(big_u[...], above[chunk], ((1,), (0,))).astype(BF16)
        part = dot(left, vu_own[cols, :], ((1,), (0,)))
        uacc[...] = part if chunk == 0 else uacc[...] + part

    for chunk in range(chunks):
        cols = slice(chunk * width, (chunk + 1) * width)
        total = wacc[:, cols] + uacc[:, cols].astype(BF16).astype(F32)
        wout[chunk] = total.reshape(ne, 24, width).astype(BF16)
        exchange(2, chunk, wout.at[chunk], warr[chunk])

    def sigma(chunk):
        cols = slice(chunk * width, (chunk + 1) * width)
        arrived(2, chunk, warr[chunk])

        def place(energy, carry):
            put_second(energy, warr[chunk][inv[energy]].astype(F32))
            return carry

        lax.fori_loop(0, ne, place, 0, unroll=4)
        for first in range(0, ne, BLK):
            def step(energy, acc):
                window = fl[chunk, pl.ds(BLK + first - energy, BLK)]
                xr, xi, yr, yi, a, b, m1, m2 = products(window, energy, acc)
                return a + (xr * yi + xi * yr), b + (xr * yr - xi * yi), m1, m2

            a, b, m1, m2 = lax.fori_loop(0, first + BLK, step, blank, unroll=4)
            mixed = jnp.where(top_rows, -(m2 + pltpu.roll(m2, 4, 1)), pltpu.roll(m1, 4, 1) - m1)
            grid_out[first : first + BLK] = jnp.concatenate([-a, b, mixed], axis=1) * scale

        def to_slot(slot, carry):
            value = grid_out[slot_ref[slot]]
            out_ref[0, slot, :, cols] = jnp.concatenate([value[0:8], value[16:20]], axis=0).astype(BF16)
            out_ref[1, slot, :, cols] = jnp.concatenate([value[8:16], value[20:24]], axis=0).astype(BF16)
            return carry

        lax.fori_loop(0, ne, to_slot, 0, unroll=4)

    for chunk in range(chunks):
        sigma(chunk)

    for copy in copies:
        copy.wait_send()
    for chunk in range(chunks):
        sent(0, chunk, green_ref.at[chunk])
        sent(1, chunk, pout.at[chunk])
        sent(2, chunk, wout.at[chunk])


def shards(ne, nb, chunks, green, v_diag, v_low, energy_slot):
    size = v_diag.shape[-1]
    width = size // chunks
    rows = 24 * ne
    packed = pack_green(green[:, 0, 0], chunks)
    vmem = pl.BlockSpec(memory_space=pltpu.VMEM)
    scratch = (
        [pltpu.VMEM((ne, 48, width), BF16)] * chunks
        + [pltpu.VMEM((ne, 24, width), BF16)] * chunks
        + [pltpu.VMEM((ne, 24, width), BF16)] * chunks
        + [
            pltpu.VMEM((chunks, ne, 24, width), BF16),
            pltpu.VMEM((chunks, ne, 24, width), BF16),
            pltpu.VMEM((chunks, rows, width), BF16),
            pltpu.VMEM((chunks, rows, width), BF16),
            pltpu.VMEM((chunks, rows, width), BF16),
            pltpu.VMEM((size, size), BF16),
            pltpu.VMEM((chunks, ne + 2 * BLK, 24, width), F32),
            pltpu.VMEM((ne, 32, width), F32),
            pltpu.VMEM((ne, 24, width), F32),
            pltpu.SMEM((ne,), jnp.int32),
            pltpu.VMEM((rows, size), BF16),
            pltpu.VMEM((rows, rows), BF16),
            pltpu.VMEM((rows, rows), BF16),
            pltpu.VMEM((rows, rows), BF16),
            pltpu.VMEM((size, size), BF16),
            pltpu.VMEM((size, size), BF16),
            pltpu.VMEM((rows, size), F32),
            pltpu.VMEM((rows, size), F32),
            pltpu.SemaphoreType.DMA((3 * chunks,)),
            pltpu.SemaphoreType.DMA((3 * chunks,)),
            pltpu.SemaphoreType.DMA((1 + 2 * chunks,)),
            pltpu.SemaphoreType.DMA((1 + 2 * chunks,)),
        ]
    )
    sigma = pl.pallas_call(
        functools.partial(kernel, ne, nb, chunks),
        out_shape=jax.ShapeDtypeStruct((2, ne, 12, size), BF16),
        in_specs=[pl.BlockSpec(memory_space=pltpu.SMEM), vmem, vmem, vmem],
        out_specs=vmem,
        scratch_shapes=scratch,
        compiler_params=pltpu.CompilerParams(
            collective_id=0, has_side_effects=True, vmem_limit_bytes=40 * 1024 * 1024
        ),
        cost_estimate=pl.CostEstimate(flops=2_500_000_000, bytes_accessed=4_000_000, transcendentals=0),
    )(energy_slot, packed, v_diag[0], v_low[0])
    return sigma[:, :, None]


def solution(mesh):
    in_specs = (
        P(None, "energy", "space", None, None),
        P("space", None, None),
        P("space", None, None),
        P(),
    )
    out_specs = P(None, None, "space", "energy", None)
    body = functools.partial(shards, mesh.shape["energy"], mesh.shape["space"], 3)
    return jax.shard_map(body, mesh=mesh, in_specs=in_specs, out_specs=out_specs, check_vma=False)
```

```python
import functools

import jax
import jax.numpy as jnp
from jax import lax
from jax.experimental import pallas as pl
from jax.experimental.pallas import tpu as pltpu
from jax.sharding import PartitionSpec as P

F32 = jnp.float32
BF16 = jnp.bfloat16
MESH = pl.DeviceIdType.MESH
BLK = 8


def pack_green(green_ref, packed, cols):
    def four_owners(quad, carry):
        rows = pl.ds(pl.multiple_of(48 * quad, 48), 48)
        parts = [green_ref[part, rows, cols].astype(F32) for part in range(4)]
        for i in range(4):
            top = [part[12 * i : 12 * i + 8] for part in parts]
            end = [part[12 * i + 8 : 12 * i + 12] for part in parts]
            value = jnp.concatenate([top[0], top[1], end[0], end[1], top[2], top[3], end[2], end[3]], axis=0)
            packed[4 * quad + i] = value.astype(BF16)
        return carry

    lax.fori_loop(0, green_ref.shape[1] // 48, four_owners, 0)


def group_index(position):
    owner = (position * 2731) >> 16
    inner = position - 24 * owner
    component = jnp.where(inner < 16, inner >> 3, (inner - 16) >> 2)
    row = jnp.where(inner < 16, inner & 7, 8 + (inner & 3))
    return component, 12 * owner + row


def dot(a, b, dims):
    return lax.dot_general(a, b, (dims, ((), ())), preferred_element_type=F32)


def kernel(ne, nb, chunks, slot_ref, green_ref, vd_ref, vl_ref, out_ref, *scratch):
    arr = scratch[0:chunks]
    abuf = scratch[chunks : 2 * chunks]
    warr = scratch[2 * chunks : 3 * chunks]
    (packed, pout, wout, own, below, above, vup, fl, fg, grid_out, inv, spread, big_d, big_l, big_u,
     vl_own, vu_own, wacc, uacc, send_sem, recv_sem, space_send, space_recv) = scratch[3 * chunks :]
    size = vd_ref.shape[0]
    width = size // chunks
    me = lax.axis_index("energy")
    here = lax.axis_index("space")
    up = lax.rem(here + 1, nb)
    down = lax.rem(here + nb - 1, nb)
    scale = ne ** -0.5

    barrier = pltpu.get_barrier_semaphore()

    def greet(step, carry):
        peer = lax.rem(me + step, ne)
        pl.semaphore_signal(barrier, inc=1, device_id={"energy": peer, "space": here}, device_id_type=MESH)
        return carry

    lax.fori_loop(1, ne, greet, 0)
    for other in (up, down):
        pl.semaphore_signal(barrier, inc=1, device_id={"energy": me, "space": other}, device_id_type=MESH)

    def pack(chunk):
        pack_green(green_ref, packed.at[chunk], slice(chunk * width, (chunk + 1) * width))

    pack(0)
    pl.semaphore_wait(barrier, ne + 1)

    def to_space(src, dst, number, other):
        return pltpu.make_async_remote_copy(
            src_ref=src, dst_ref=dst, send_sem=space_send.at[number], recv_sem=space_recv.at[number],
            device_id={"energy": me, "space": other}, device_id_type=MESH)

    def exchange(phase, chunk, src, dst):
        number = phase * chunks + chunk

        def send(step, carry):
            peer = lax.rem(me + step, ne)
            pltpu.make_async_remote_copy(
                src_ref=src.at[peer], dst_ref=dst.at[me], send_sem=send_sem.at[number],
                recv_sem=recv_sem.at[number], device_id={"energy": peer, "space": here},
                device_id_type=MESH).start()
            return carry

        lax.fori_loop(1, ne, send, 0)
        pltpu.make_async_copy(src.at[me], dst.at[me], recv_sem.at[number]).start()

    def arrived(phase, chunk, dst):
        pltpu.make_async_copy(dst, dst, recv_sem.at[phase * chunks + chunk]).wait()

    def sent(phase, chunk, src):
        part = src.at[pl.ds(0, ne - 1)]
        pltpu.make_async_copy(part, part, send_sem.at[phase * chunks + chunk]).wait()

    exchange(0, 0, packed.at[0], arr[0])
    for chunk in range(1, min(2, chunks)):
        pack(chunk)
        exchange(0, chunk, packed.at[chunk], arr[chunk])
    coupling = to_space(vl_ref, vup, 0, down)
    coupling.start()
    for chunk in range(2, chunks):
        pack(chunk)

    def invert(energy, carry):
        def look(slot, found):
            return jnp.where(slot_ref[slot] == energy, slot, found)

        inv[energy] = lax.fori_loop(0, ne, look, 0)
        return carry

    lax.fori_loop(0, ne, invert, 0)

    rows = 24 * ne
    _, row_of = group_index(lax.broadcasted_iota(jnp.int32, (rows, size), 0))
    spread[...] = jnp.where(row_of == lax.broadcasted_iota(jnp.int32, (rows, size), 1), 1.0, 0.0).astype(BF16)
    comp_a, _ = group_index(lax.broadcasted_iota(jnp.int32, (rows, rows), 0))
    comp_b, _ = group_index(lax.broadcasted_iota(jnp.int32, (rows, rows), 1))
    same = comp_a == comp_b

    def expand(matrix, dims):
        half = dot(spread[...], matrix, dims).astype(BF16)
        return jnp.where(same, dot(half, spread[...], ((1,), (1,))), 0.0).astype(BF16)

    big_d[...] = expand(vd_ref[...], ((1,), (0,)))
    vl_own[...] = jnp.where(here > 0, vl_ref[...], jnp.zeros_like(vl_ref))
    big_l[...] = expand(vl_own[...], ((1,), (0,)))

    zeros = jnp.zeros((BLK, 24, width), F32)
    for chunk in range(chunks):
        fl[chunk, 0:BLK] = zeros
        fl[chunk, BLK + ne : 2 * BLK + ne] = zeros
    top_rows = lax.broadcasted_iota(jnp.int32, (BLK, 8, width), 1) < 4

    def put_second(energy, value):
        fg[energy, 0:24] = value
        fg[energy, 24:32] = pltpu.roll(value[16:24], 4, 0)

    def products(window, energy, acc):
        a, b, m1, m2 = acc
        xr, xi, xm = window[:, 0:8], window[:, 8:16], window[:, 16:24]
        second = fg[energy]
        yr, yi, ym, ys = (second[8 * i : 8 * i + 8][None] for i in range(4))
        return xr, xi, yr, yi, a, b, m1 + xm * ym, m2 + xm * ys

    blank = tuple(jnp.zeros((BLK, 8, width), F32) for _ in range(4))

    def polar(chunk):
        arrived(0, chunk, arr[chunk])

        def place(energy, carry):
            value = arr[chunk][inv[energy]].astype(F32)
            fl[chunk, BLK + energy] = value[0:24]
            put_second(energy, value[24:48])
            return carry

        lax.fori_loop(0, ne, place, 0, unroll=4)
        for first in range(0, ne, BLK):
            def step(energy, acc):
                window = fl[chunk, pl.ds(BLK + first + energy, BLK)]
                xr, xi, yr, yi, a, b, m1, m2 = products(window, energy, acc)
                return a + (xi * yr - xr * yi), b + (xr * yr + xi * yi), m1, m2

            a, b, m1, m2 = lax.fori_loop(0, ne - first, step, blank, unroll=4)
            mixed = jnp.where(top_rows, pltpu.roll(m2, 4, 1) - m2, -(m1 + pltpu.roll(m1, 4, 1)))
            grid_out[first : first + BLK] = jnp.concatenate([a, -b, mixed], axis=1) * scale

        def to_slot(slot, carry):
            pout[chunk, slot] = grid_out[slot_ref[slot]].astype(BF16)
            return carry

        lax.fori_loop(0, ne, to_slot, 0, unroll=4)
        exchange(1, chunk, pout.at[chunk], abuf[chunk])

    copies = []

    def pass_on(chunk):
        arrived(1, chunk, abuf[chunk])
        own[chunk] = abuf[chunk][...].astype(F32).reshape(rows, width).astype(BF16)
        for number, dst, other in ((1 + chunk, below, up), (1 + chunks + chunk, above, down)):
            copy = to_space(own.at[chunk], dst.at[chunk], number, other)
            copy.start()
            copies.append(copy)

    def own_products(chunk):
        cols = slice(chunk * width, (chunk + 1) * width)
        left = dot(big_d[...], own[chunk], ((1,), (0,))).astype(BF16)
        part = dot(left, vd_ref[:, cols], ((1,), (1,)))
        wacc[...] = part if chunk == 0 else wacc[...] + part

    for chunk in range(chunks):
        polar(chunk)
        if chunk + 2 < chunks:
            exchange(0, chunk + 2, packed.at[chunk + 2], arr[chunk + 2])
        if chunk > 0:
            pass_on(chunk - 1)

    coupling.wait()
    vu_own[...] = jnp.where(here < nb - 1, vup[...], jnp.zeros_like(vup))
    big_u[...] = expand(vu_own[...], ((1,), (1,)))
    pass_on(chunks - 1)
    for chunk in range(chunks):
        own_products(chunk)

    for chunk in range(chunks):
        cols = slice(chunk * width, (chunk + 1) * width)
        copies[2 * chunk].wait_recv()
        left = dot(big_l[...], below[chunk], ((1,), (0,))).astype(BF16)
        wacc[...] += dot(left, vl_own[:, cols], ((1,), (1,)))
        copies[2 * chunk + 1].wait_recv()
        left = dot(big_u[...], above[chunk], ((1,), (0,))).astype(BF16)
        part = dot(left, vu_own[cols, :], ((1,), (0,)))
        uacc[...] = part if chunk == 0 else uacc[...] + part

    for chunk in range(chunks):
        cols = slice(chunk * width, (chunk + 1) * width)
        total = wacc[:, cols] + uacc[:, cols].astype(BF16).astype(F32)
        wout[chunk] = total.reshape(ne, 24, width).astype(BF16)
        exchange(2, chunk, wout.at[chunk], warr[chunk])

    def sigma(chunk):
        cols = slice(chunk * width, (chunk + 1) * width)
        arrived(2, chunk, warr[chunk])

        def place(energy, carry):
            put_second(energy, warr[chunk][inv[energy]].astype(F32))
            return carry

        lax.fori_loop(0, ne, place, 0, unroll=4)
        for first in range(0, ne, BLK):
            def step(energy, acc):
                window = fl[chunk, pl.ds(BLK + first - energy, BLK)]
                xr, xi, yr, yi, a, b, m1, m2 = products(window, energy, acc)
                return a + (xr * yi + xi * yr), b + (xr * yr - xi * yi), m1, m2

            a, b, m1, m2 = lax.fori_loop(0, first + BLK, step, blank, unroll=4)
            mixed = jnp.where(top_rows, -(m2 + pltpu.roll(m2, 4, 1)), pltpu.roll(m1, 4, 1) - m1)
            grid_out[first : first + BLK] = jnp.concatenate([-a, b, mixed], axis=1) * scale

        def to_slot(slot, carry):
            value = grid_out[slot_ref[slot]]
            out_ref[0, slot, :, cols] = jnp.concatenate([value[0:8], value[16:20]], axis=0).astype(BF16)
            out_ref[1, slot, :, cols] = jnp.concatenate([value[8:16], value[20:24]], axis=0).astype(BF16)
            return carry

        lax.fori_loop(0, ne, to_slot, 0, unroll=4)

    for chunk in range(chunks):
        sigma(chunk)

    for copy in copies:
        copy.wait_send()
    for chunk in range(chunks):
        sent(0, chunk, packed.at[chunk])
        sent(1, chunk, pout.at[chunk])
        sent(2, chunk, wout.at[chunk])


def shards(ne, nb, chunks, green, v_diag, v_low, energy_slot):
    size = v_diag.shape[-1]
    width = size // chunks
    rows = 24 * ne
    vmem = pl.BlockSpec(memory_space=pltpu.VMEM)
    scratch = (
        [pltpu.VMEM((ne, 48, width), BF16)] * chunks
        + [pltpu.VMEM((ne, 24, width), BF16)] * chunks
        + [pltpu.VMEM((ne, 24, width), BF16)] * chunks
        + [
            pltpu.VMEM((chunks, ne, 48, width), BF16),
            pltpu.VMEM((chunks, ne, 24, width), BF16),
            pltpu.VMEM((chunks, ne, 24, width), BF16),
            pltpu.VMEM((chunks, rows, width), BF16),
            pltpu.VMEM((chunks, rows, width), BF16),
            pltpu.VMEM((chunks, rows, width), BF16),
            pltpu.VMEM((size, size), BF16),
            pltpu.VMEM((chunks, ne + 2 * BLK, 24, width), F32),
            pltpu.VMEM((ne, 32, width), F32),
            pltpu.VMEM((ne, 24, width), F32),
            pltpu.SMEM((ne,), jnp.int32),
            pltpu.VMEM((rows, size), BF16),
            pltpu.VMEM((rows, rows), BF16),
            pltpu.VMEM((rows, rows), BF16),
            pltpu.VMEM((rows, rows), BF16),
            pltpu.VMEM((size, size), BF16),
            pltpu.VMEM((size, size), BF16),
            pltpu.VMEM((rows, size), F32),
            pltpu.VMEM((rows, size), F32),
            pltpu.SemaphoreType.DMA((3 * chunks,)),
            pltpu.SemaphoreType.DMA((3 * chunks,)),
            pltpu.SemaphoreType.DMA((1 + 2 * chunks,)),
            pltpu.SemaphoreType.DMA((1 + 2 * chunks,)),
        ]
    )
    sigma = pl.pallas_call(
        functools.partial(kernel, ne, nb, chunks),
        out_shape=jax.ShapeDtypeStruct((2, ne, 12, size), BF16),
        in_specs=[pl.BlockSpec(memory_space=pltpu.SMEM), vmem, vmem, vmem],
        out_specs=vmem,
        scratch_shapes=scratch,
        compiler_params=pltpu.CompilerParams(
            collective_id=0, has_side_effects=True, vmem_limit_bytes=40 * 1024 * 1024
        ),
        cost_estimate=pl.CostEstimate(flops=2_500_000_000, bytes_accessed=4_000_000, transcendentals=0),
    )(energy_slot, green[:, 0, 0], v_diag[0], v_low[0])
    return sigma[:, :, None]


def solution(mesh):
    in_specs = (
        P(None, "energy", "space", None, None),
        P("space", None, None),
        P("space", None, None),
        P(),
    )
    out_specs = P(None, None, "space", "energy", None)
    body = functools.partial(shards, mesh.shape["energy"], mesh.shape["space"], 3)
    return jax.shard_map(body, mesh=mesh, in_specs=in_specs, out_specs=out_specs, check_vma=False)
```

```python
import functools

import jax
import jax.numpy as jnp
from jax import lax
from jax.experimental import pallas as pl
from jax.experimental.pallas import tpu as pltpu
from jax.sharding import PartitionSpec as P

F32 = jnp.float32
BF16 = jnp.bfloat16
MESH = pl.DeviceIdType.MESH
BLK = 8


def pack_green(green_ref, packed, cols):
    def four_owners(quad, carry):
        rows = pl.ds(pl.multiple_of(48 * quad, 48), 48)
        parts = [green_ref[part, rows, cols].astype(F32) for part in range(4)]
        for i in range(4):
            top = [part[12 * i : 12 * i + 8] for part in parts]
            end = [part[12 * i + 8 : 12 * i + 12] for part in parts]
            value = jnp.concatenate([top[0], top[1], end[0], end[1], top[2], top[3], end[2], end[3]], axis=0)
            packed[4 * quad + i] = value.astype(BF16)
        return carry

    lax.fori_loop(0, green_ref.shape[1] // 48, four_owners, 0)


def group_index(position):
    owner = (position * 2731) >> 16
    inner = position - 24 * owner
    component = jnp.where(inner < 16, inner >> 3, (inner - 16) >> 2)
    row = jnp.where(inner < 16, inner & 7, 8 + (inner & 3))
    return component, 12 * owner + row


def dot(a, b, dims):
    return lax.dot_general(a, b, (dims, ((), ())), preferred_element_type=F32)


def kernel(ne, nb, chunks, slot_ref, green_hbm, vd_hbm, vl_hbm, out_ref, *scratch):
    arr = scratch[0:chunks]
    abuf = scratch[chunks : 2 * chunks]
    warr = scratch[2 * chunks : 3 * chunks]
    (green_ref, vd_ref, vl_ref, local_sem, packed, pout, wout, own, below, above, vup, fl, fg, grid_out, inv, spread, big_d, big_l, big_u,
     vl_own, vu_own, wacc, uacc, send_sem, recv_sem, space_send, space_recv) = scratch[3 * chunks :]
    size = vd_ref.shape[0]
    width = size // chunks
    me = lax.axis_index("energy")
    here = lax.axis_index("space")
    up = lax.rem(here + 1, nb)
    down = lax.rem(here + nb - 1, nb)
    scale = ne ** -0.5

    loads = [
        pltpu.make_async_copy(src, dst, local_sem.at[i])
        for i, (src, dst) in enumerate(((green_hbm, green_ref), (vd_hbm, vd_ref), (vl_hbm, vl_ref)))
    ]
    for load in loads:
        load.start()

    barrier = pltpu.get_barrier_semaphore()

    def greet(step, carry):
        peer = lax.rem(me + step, ne)
        pl.semaphore_signal(barrier, inc=1, device_id={"energy": peer, "space": here}, device_id_type=MESH)
        return carry

    lax.fori_loop(1, ne, greet, 0)
    for other in (up, down):
        pl.semaphore_signal(barrier, inc=1, device_id={"energy": me, "space": other}, device_id_type=MESH)

    def pack(chunk):
        pack_green(green_ref, packed.at[chunk], slice(chunk * width, (chunk + 1) * width))

    loads[0].wait()
    pack(0)
    pl.semaphore_wait(barrier, ne + 1)

    def to_space(src, dst, number, other):
        return pltpu.make_async_remote_copy(
            src_ref=src, dst_ref=dst, send_sem=space_send.at[number], recv_sem=space_recv.at[number],
            device_id={"energy": me, "space": other}, device_id_type=MESH)

    def exchange(phase, chunk, src, dst):
        number = phase * chunks + chunk

        def send(step, carry):
            peer = lax.rem(me + step, ne)
            pltpu.make_async_remote_copy(
                src_ref=src.at[peer], dst_ref=dst.at[me], send_sem=send_sem.at[number],
                recv_sem=recv_sem.at[number], device_id={"energy": peer, "space": here},
                device_id_type=MESH).start()
            return carry

        lax.fori_loop(1, ne, send, 0)
        pltpu.make_async_copy(src.at[me], dst.at[me], recv_sem.at[number]).start()

    def arrived(phase, chunk, dst):
        pltpu.make_async_copy(dst, dst, recv_sem.at[phase * chunks + chunk]).wait()

    def sent(phase, chunk, src):
        part = src.at[pl.ds(0, ne - 1)]
        pltpu.make_async_copy(part, part, send_sem.at[phase * chunks + chunk]).wait()

    exchange(0, 0, packed.at[0], arr[0])
    for chunk in range(1, min(2, chunks)):
        pack(chunk)
        exchange(0, chunk, packed.at[chunk], arr[chunk])
    core = lax.rem(me, 2)
    half = pl.ds(pl.multiple_of(core * (size // 2), size // 2), size // 2)
    coupling = to_space(vl_hbm.at[half], vup.at[half], 0, down)
    coupling.start()
    swap = pltpu.make_async_remote_copy(
        src_ref=vup.at[half], dst_ref=vup.at[half], send_sem=space_send.at[1 + 2 * chunks],
        recv_sem=space_recv.at[1 + 2 * chunks], device_id={"energy": me + 1 - 2 * core, "space": here},
        device_id_type=MESH)
    for chunk in range(2, chunks):
        pack(chunk)

    def invert(energy, carry):
        def look(slot, found):
            return jnp.where(slot_ref[slot] == energy, slot, found)

        inv[energy] = lax.fori_loop(0, ne, look, 0)
        return carry

    lax.fori_loop(0, ne, invert, 0)

    rows = 24 * ne
    comp_a, _ = group_index(lax.broadcasted_iota(jnp.int32, (rows, rows), 0))
    comp_b, _ = group_index(lax.broadcasted_iota(jnp.int32, (rows, rows), 1))
    same = comp_a == comp_b

    def expand(matrix, dims):
        half = dot(spread[...], matrix, dims).astype(BF16)
        return jnp.where(same, dot(half, spread[...], ((1,), (1,))), 0.0).astype(BF16)

    def prepare():
        _, row_of = group_index(lax.broadcasted_iota(jnp.int32, (rows, size), 0))
        spread[...] = jnp.where(row_of == lax.broadcasted_iota(jnp.int32, (rows, size), 1), 1.0, 0.0).astype(BF16)
        loads[1].wait()
        loads[2].wait()
        big_d[...] = expand(vd_ref[...], ((1,), (0,)))
        vl_own[...] = jnp.where(here > 0, vl_ref[...], jnp.zeros_like(vl_ref))
        big_l[...] = expand(vl_own[...], ((1,), (0,)))


    zeros = jnp.zeros((BLK, 24, width), F32)
    for chunk in range(chunks):
        fl[chunk, 0:BLK] = zeros
        fl[chunk, BLK + ne : 2 * BLK + ne] = zeros
    top_rows = lax.broadcasted_iota(jnp.int32, (BLK, 8, width), 1) < 4

    def put_second(energy, value):
        fg[energy, 0:24] = value
        fg[energy, 24:32] = pltpu.roll(value[16:24], 4, 0)

    def products(window, energy, acc):
        a, b, m1, m2 = acc
        xr, xi, xm = window[:, 0:8], window[:, 8:16], window[:, 16:24]
        second = fg[energy]
        yr, yi, ym, ys = (second[8 * i : 8 * i + 8][None] for i in range(4))
        return xr, xi, yr, yi, a, b, m1 + xm * ym, m2 + xm * ys

    blank = tuple(jnp.zeros((BLK, 8, width), F32) for _ in range(4))

    def polar(chunk):
        arrived(0, chunk, arr[chunk])

        def place(energy, carry):
            value = arr[chunk][inv[energy]].astype(F32)
            fl[chunk, BLK + energy] = value[0:24]
            put_second(energy, value[24:48])
            return carry

        lax.fori_loop(0, ne, place, 0, unroll=4)
        for first in range(0, ne, BLK):
            def step(energy, acc):
                window = fl[chunk, pl.ds(BLK + first + energy, BLK)]
                xr, xi, yr, yi, a, b, m1, m2 = products(window, energy, acc)
                return a + (xi * yr - xr * yi), b + (xr * yr + xi * yi), m1, m2

            a, b, m1, m2 = lax.fori_loop(0, ne - first, step, blank, unroll=4)
            mixed = jnp.where(top_rows, pltpu.roll(m2, 4, 1) - m2, -(m1 + pltpu.roll(m1, 4, 1)))
            grid_out[first : first + BLK] = jnp.concatenate([a, -b, mixed], axis=1) * scale

        def to_slot(slot, carry):
            pout[chunk, slot] = grid_out[slot_ref[slot]].astype(BF16)
            return carry

        lax.fori_loop(0, ne, to_slot, 0, unroll=4)
        exchange(1, chunk, pout.at[chunk], abuf[chunk])

    copies = []

    def pass_on(chunk):
        arrived(1, chunk, abuf[chunk])
        own[chunk] = abuf[chunk][...].astype(F32).reshape(rows, width).astype(BF16)
        for number, dst, other in ((1 + chunk, below, up), (1 + chunks + chunk, above, down)):
            copy = to_space(own.at[chunk], dst.at[chunk], number, other)
            copy.start()
            copies.append(copy)

    def own_products(chunk):
        cols = slice(chunk * width, (chunk + 1) * width)
        left = dot(big_d[...], own[chunk], ((1,), (0,))).astype(BF16)
        part = dot(left, vd_ref[:, cols], ((1,), (1,)))
        wacc[...] = part if chunk == 0 else wacc[...] + part

    for chunk in range(chunks):
        polar(chunk)
        if chunk + 2 < chunks:
            exchange(0, chunk + 2, packed.at[chunk + 2], arr[chunk + 2])
        if chunk == 0:
            prepare()
        if chunk > 0:
            pass_on(chunk - 1)
        if chunk == 1:
            coupling.wait()
            swap.start()

    swap.wait()
    vu_own[...] = jnp.where(here < nb - 1, vup[...], jnp.zeros_like(vup))
    big_u[...] = expand(vu_own[...], ((1,), (1,)))
    pass_on(chunks - 1)
    for chunk in range(chunks):
        own_products(chunk)

    for chunk in range(chunks):
        cols = slice(chunk * width, (chunk + 1) * width)
        copies[2 * chunk].wait_recv()
        left = dot(big_l[...], below[chunk], ((1,), (0,))).astype(BF16)
        wacc[...] += dot(left, vl_own[:, cols], ((1,), (1,)))
        copies[2 * chunk + 1].wait_recv()
        left = dot(big_u[...], above[chunk], ((1,), (0,))).astype(BF16)
        part = dot(left, vu_own[cols, :], ((1,), (0,)))
        uacc[...] = part if chunk == 0 else uacc[...] + part

    for chunk in range(chunks):
        cols = slice(chunk * width, (chunk + 1) * width)
        total = wacc[:, cols] + uacc[:, cols].astype(BF16).astype(F32)
        wout[chunk] = total.reshape(ne, 24, width).astype(BF16)
        exchange(2, chunk, wout.at[chunk], warr[chunk])

    def sigma(chunk):
        cols = slice(chunk * width, (chunk + 1) * width)
        arrived(2, chunk, warr[chunk])

        def place(energy, carry):
            put_second(energy, warr[chunk][inv[energy]].astype(F32))
            return carry

        lax.fori_loop(0, ne, place, 0, unroll=4)
        for first in range(0, ne, BLK):
            def step(energy, acc):
                window = fl[chunk, pl.ds(BLK + first - energy, BLK)]
                xr, xi, yr, yi, a, b, m1, m2 = products(window, energy, acc)
                return a + (xr * yi + xi * yr), b + (xr * yr - xi * yi), m1, m2

            a, b, m1, m2 = lax.fori_loop(0, first + BLK, step, blank, unroll=4)
            mixed = jnp.where(top_rows, -(m2 + pltpu.roll(m2, 4, 1)), pltpu.roll(m1, 4, 1) - m1)
            grid_out[first : first + BLK] = jnp.concatenate([-a, b, mixed], axis=1) * scale

        def to_slot(slot, carry):
            value = grid_out[slot_ref[slot]]
            out_ref[0, slot, :, cols] = jnp.concatenate([value[0:8], value[16:20]], axis=0).astype(BF16)
            out_ref[1, slot, :, cols] = jnp.concatenate([value[8:16], value[20:24]], axis=0).astype(BF16)
            return carry

        lax.fori_loop(0, ne, to_slot, 0, unroll=4)

    for chunk in range(chunks):
        sigma(chunk)

    for copy in copies:
        copy.wait_send()
    for chunk in range(chunks):
        sent(0, chunk, packed.at[chunk])
        sent(1, chunk, pout.at[chunk])
        sent(2, chunk, wout.at[chunk])


def shards(ne, nb, chunks, green, v_diag, v_low, energy_slot):
    size = v_diag.shape[-1]
    width = size // chunks
    rows = 24 * ne
    vmem = pl.BlockSpec(memory_space=pltpu.VMEM)
    hbm = pl.BlockSpec(memory_space=pltpu.HBM)
    scratch = (
        [pltpu.VMEM((ne, 48, width), BF16)] * chunks
        + [pltpu.VMEM((ne, 24, width), BF16)] * chunks
        + [pltpu.VMEM((ne, 24, width), BF16)] * chunks
        + [
            pltpu.VMEM((4, size, size), BF16),
            pltpu.VMEM((size, size), BF16),
            pltpu.VMEM((size, size), BF16),
            pltpu.SemaphoreType.DMA((3,)),
            pltpu.VMEM((chunks, ne, 48, width), BF16),
            pltpu.VMEM((chunks, ne, 24, width), BF16),
            pltpu.VMEM((chunks, ne, 24, width), BF16),
            pltpu.VMEM((chunks, rows, width), BF16),
            pltpu.VMEM((chunks, rows, width), BF16),
            pltpu.VMEM((chunks, rows, width), BF16),
            pltpu.VMEM((size, size), BF16),
            pltpu.VMEM((chunks, ne + 2 * BLK, 24, width), F32),
            pltpu.VMEM((ne, 32, width), F32),
            pltpu.VMEM((ne, 24, width), F32),
            pltpu.SMEM((ne,), jnp.int32),
            pltpu.VMEM((rows, size), BF16),
            pltpu.VMEM((rows, rows), BF16),
            pltpu.VMEM((rows, rows), BF16),
            pltpu.VMEM((rows, rows), BF16),
            pltpu.VMEM((size, size), BF16),
            pltpu.VMEM((size, size), BF16),
            pltpu.VMEM((rows, size), F32),
            pltpu.VMEM((rows, size), F32),
            pltpu.SemaphoreType.DMA((3 * chunks,)),
            pltpu.SemaphoreType.DMA((3 * chunks,)),
            pltpu.SemaphoreType.DMA((2 + 2 * chunks,)),
            pltpu.SemaphoreType.DMA((2 + 2 * chunks,)),
        ]
    )
    sigma = pl.pallas_call(
        functools.partial(kernel, ne, nb, chunks),
        out_shape=jax.ShapeDtypeStruct((2, ne, 12, size), BF16),
        in_specs=[pl.BlockSpec(memory_space=pltpu.SMEM), hbm, hbm, hbm],
        out_specs=vmem,
        scratch_shapes=scratch,
        compiler_params=pltpu.CompilerParams(
            collective_id=0, has_side_effects=True, vmem_limit_bytes=56 * 1024 * 1024
        ),
        cost_estimate=pl.CostEstimate(flops=2_500_000_000, bytes_accessed=4_000_000, transcendentals=0),
    )(energy_slot, green[:, 0, 0], v_diag[0], v_low[0])
    return sigma[:, :, None]


def solution(mesh):
    in_specs = (
        P(None, "energy", "space", None, None),
        P("space", None, None),
        P("space", None, None),
        P(),
    )
    out_specs = P(None, None, "space", "energy", None)
    body = functools.partial(shards, mesh.shape["energy"], mesh.shape["space"], 3)
    return jax.shard_map(body, mesh=mesh, in_specs=in_specs, out_specs=out_specs, check_vma=False)
```

```python
import functools

import jax
import jax.numpy as jnp
from jax import lax
from jax.experimental import pallas as pl
from jax.experimental.pallas import tpu as pltpu
from jax.sharding import PartitionSpec as P

F32 = jnp.float32
BF16 = jnp.bfloat16
MESH = pl.DeviceIdType.MESH
BLK = 8


def pack_green(green_ref, packed, cols):
    def four_owners(quad, carry):
        rows = pl.ds(pl.multiple_of(48 * quad, 48), 48)
        parts = [green_ref[part, rows, cols].astype(F32) for part in range(4)]
        for i in range(4):
            top = [part[12 * i : 12 * i + 8] for part in parts]
            end = [part[12 * i + 8 : 12 * i + 12] for part in parts]
            value = jnp.concatenate([top[0], top[1], end[0], end[1], top[2], top[3], end[2], end[3]], axis=0)
            packed[4 * quad + i] = value.astype(BF16)
        return carry

    lax.fori_loop(0, green_ref.shape[1] // 48, four_owners, 0)


def group_index(position):
    owner = (position * 2731) >> 16
    inner = position - 24 * owner
    component = jnp.where(inner < 16, inner >> 3, (inner - 16) >> 2)
    row = jnp.where(inner < 16, inner & 7, 8 + (inner & 3))
    return component, 12 * owner + row


def dot(a, b, dims):
    return lax.dot_general(a, b, (dims, ((), ())), preferred_element_type=F32)


def kernel(ne, nb, chunks, slot_ref, green_hbm, vd_hbm, vl_hbm, out_ref, *scratch):
    arr = scratch[0:chunks]
    abuf = scratch[chunks : 2 * chunks]
    warr = scratch[2 * chunks : 3 * chunks]
    (green_ref, vd_ref, vl_ref, local_sem, packed, pout, wout, own, below, above, vup, fl, fg, grid_out, inv, spread, big_d, big_l, big_u,
     vl_own, vu_own, wacc, uacc, send_sem, recv_sem, space_send, space_recv) = scratch[3 * chunks :]
    size = vd_ref.shape[0]
    width = size // chunks
    me = lax.axis_index("energy")
    here = lax.axis_index("space")
    up = lax.rem(here + 1, nb)
    down = lax.rem(here + nb - 1, nb)
    scale = ne ** -0.5

    loads = [
        pltpu.make_async_copy(src, dst, local_sem.at[i])
        for i, (src, dst) in enumerate(((green_hbm, green_ref), (vd_hbm, vd_ref), (vl_hbm, vl_ref)))
    ]
    for load in loads:
        load.start()

    barrier = pltpu.get_barrier_semaphore()

    def greet(step, carry):
        peer = lax.rem(me + step, ne)
        pl.semaphore_signal(barrier, inc=1, device_id={"energy": peer, "space": here}, device_id_type=MESH)
        return carry

    lax.fori_loop(1, ne, greet, 0)
    for other in (up, down):
        pl.semaphore_signal(barrier, inc=1, device_id={"energy": me, "space": other}, device_id_type=MESH)

    def pack(chunk):
        pack_green(green_ref, packed.at[chunk], slice(chunk * width, (chunk + 1) * width))

    loads[0].wait()
    pack(0)
    pl.semaphore_wait(barrier, ne + 1)

    def to_space(src, dst, number, other):
        return pltpu.make_async_remote_copy(
            src_ref=src, dst_ref=dst, send_sem=space_send.at[number], recv_sem=space_recv.at[number],
            device_id={"energy": me, "space": other}, device_id_type=MESH)

    def exchange(phase, chunk, src, dst):
        number = phase * chunks + chunk

        def send(step, carry):
            peer = lax.rem(me + step, ne)
            pltpu.make_async_remote_copy(
                src_ref=src.at[peer], dst_ref=dst.at[me], send_sem=send_sem.at[number],
                recv_sem=recv_sem.at[number], device_id={"energy": peer, "space": here},
                device_id_type=MESH).start()
            return carry

        lax.fori_loop(1, ne, send, 0)
        pltpu.make_async_copy(src.at[me], dst.at[me], recv_sem.at[number]).start()

    def arrived(phase, chunk, dst):
        pltpu.make_async_copy(dst, dst, recv_sem.at[phase * chunks + chunk]).wait()

    def sent(phase, chunk, src):
        part = src.at[pl.ds(0, ne - 1)]
        pltpu.make_async_copy(part, part, send_sem.at[phase * chunks + chunk]).wait()

    exchange(0, 0, packed.at[0], arr[0])
    for chunk in range(1, min(2, chunks)):
        pack(chunk)
        exchange(0, chunk, packed.at[chunk], arr[chunk])
    core = lax.rem(me, 2)
    half = pl.ds(pl.multiple_of(core * (size // 2), size // 2), size // 2)
    coupling = to_space(vl_hbm.at[half], vup.at[half], 0, down)
    coupling.start()
    swap = pltpu.make_async_remote_copy(
        src_ref=vup.at[half], dst_ref=vup.at[half], send_sem=space_send.at[1 + 2 * chunks],
        recv_sem=space_recv.at[1 + 2 * chunks], device_id={"energy": me + 1 - 2 * core, "space": here},
        device_id_type=MESH)
    for chunk in range(2, chunks):
        pack(chunk)

    def invert(energy, carry):
        def look(slot, found):
            return jnp.where(slot_ref[slot] == energy, slot, found)

        inv[energy] = lax.fori_loop(0, ne, look, 0)
        return carry

    lax.fori_loop(0, ne, invert, 0)

    rows = 24 * ne
    comp_a, _ = group_index(lax.broadcasted_iota(jnp.int32, (rows, rows), 0))
    comp_b, _ = group_index(lax.broadcasted_iota(jnp.int32, (rows, rows), 1))
    same = comp_a == comp_b

    def expand(matrix, dims):
        half = dot(spread[...], matrix, dims).astype(BF16)
        return jnp.where(same, dot(half, spread[...], ((1,), (1,))), 0.0).astype(BF16)

    def prepare():
        _, row_of = group_index(lax.broadcasted_iota(jnp.int32, (rows, size), 0))
        spread[...] = jnp.where(row_of == lax.broadcasted_iota(jnp.int32, (rows, size), 1), 1.0, 0.0).astype(BF16)
        loads[1].wait()
        loads[2].wait()
        big_d[...] = expand(vd_ref[...], ((1,), (0,)))
        vl_own[...] = jnp.where(here > 0, vl_ref[...], jnp.zeros_like(vl_ref))
        big_l[...] = expand(vl_own[...], ((1,), (0,)))


    zeros = jnp.zeros((BLK, 24, width), F32)
    for chunk in range(chunks):
        fl[chunk, 0:BLK] = zeros
        fl[chunk, BLK + ne : 2 * BLK + ne] = zeros
    top_rows = lax.broadcasted_iota(jnp.int32, (BLK, 8, width), 1) < 4

    def put_second(energy, value):
        fg[energy, 0:24] = value
        fg[energy, 24:32] = pltpu.roll(value[16:24], 4, 0)

    def products(window, energy, acc):
        a, b, m1, m2 = acc
        xr, xi, xm = window[:, 0:8], window[:, 8:16], window[:, 16:24]
        second = fg[energy]
        yr, yi, ym, ys = (second[8 * i : 8 * i + 8][None] for i in range(4))
        return xr, xi, yr, yi, a, b, m1 + xm * ym, m2 + xm * ys

    blank = tuple(jnp.zeros((BLK, 8, width), F32) for _ in range(4))

    def polar(chunk):
        arrived(0, chunk, arr[chunk])

        def place(energy, carry):
            value = arr[chunk][inv[energy]].astype(F32)
            fl[chunk, BLK + energy] = value[0:24]
            put_second(energy, value[24:48])
            return carry

        lax.fori_loop(0, ne, place, 0, unroll=8)
        for first in range(0, ne, BLK):
            def step(energy, acc):
                window = fl[chunk, pl.ds(BLK + first + energy, BLK)]
                xr, xi, yr, yi, a, b, m1, m2 = products(window, energy, acc)
                return a + (xi * yr - xr * yi), b + (xr * yr + xi * yi), m1, m2

            a, b, m1, m2 = lax.fori_loop(0, ne - first, step, blank, unroll=8)
            mixed = jnp.where(top_rows, pltpu.roll(m2, 4, 1) - m2, -(m1 + pltpu.roll(m1, 4, 1)))
            grid_out[first : first + BLK] = jnp.concatenate([a, -b, mixed], axis=1) * scale

        def to_slot(slot, carry):
            pout[chunk, slot] = grid_out[slot_ref[slot]].astype(BF16)
            return carry

        lax.fori_loop(0, ne, to_slot, 0, unroll=8)
        exchange(1, chunk, pout.at[chunk], abuf[chunk])

    copies = []

    def pass_on(chunk):
        arrived(1, chunk, abuf[chunk])
        own[chunk] = abuf[chunk][...].astype(F32).reshape(rows, width).astype(BF16)
        for number, dst, other in ((1 + chunk, below, up), (1 + chunks + chunk, above, down)):
            copy = to_space(own.at[chunk], dst.at[chunk], number, other)
            copy.start()
            copies.append(copy)

    def own_products(chunk):
        cols = slice(chunk * width, (chunk + 1) * width)
        left = dot(big_d[...], own[chunk], ((1,), (0,))).astype(BF16)
        part = dot(left, vd_ref[:, cols], ((1,), (1,)))
        wacc[...] = part if chunk == 0 else wacc[...] + part

    for chunk in range(chunks):
        polar(chunk)
        if chunk + 2 < chunks:
            exchange(0, chunk + 2, packed.at[chunk + 2], arr[chunk + 2])
        if chunk == 0:
            prepare()
        if chunk > 0:
            pass_on(chunk - 1)
        if chunk == 1:
            coupling.wait()
            swap.start()

    swap.wait()
    vu_own[...] = jnp.where(here < nb - 1, vup[...], jnp.zeros_like(vup))
    big_u[...] = expand(vu_own[...], ((1,), (1,)))
    pass_on(chunks - 1)
    for chunk in range(chunks):
        own_products(chunk)

    for chunk in range(chunks):
        cols = slice(chunk * width, (chunk + 1) * width)
        copies[2 * chunk].wait_recv()
        left = dot(big_l[...], below[chunk], ((1,), (0,))).astype(BF16)
        wacc[...] += dot(left, vl_own[:, cols], ((1,), (1,)))
        copies[2 * chunk + 1].wait_recv()
        left = dot(big_u[...], above[chunk], ((1,), (0,))).astype(BF16)
        part = dot(left, vu_own[cols, :], ((1,), (0,)))
        uacc[...] = part if chunk == 0 else uacc[...] + part

    for chunk in range(chunks):
        cols = slice(chunk * width, (chunk + 1) * width)
        total = wacc[:, cols] + uacc[:, cols].astype(BF16).astype(F32)
        wout[chunk] = total.reshape(ne, 24, width).astype(BF16)
        exchange(2, chunk, wout.at[chunk], warr[chunk])

    def sigma(chunk):
        cols = slice(chunk * width, (chunk + 1) * width)
        arrived(2, chunk, warr[chunk])

        def place(energy, carry):
            put_second(energy, warr[chunk][inv[energy]].astype(F32))
            return carry

        lax.fori_loop(0, ne, place, 0, unroll=8)
        for first in range(0, ne, BLK):
            def step(energy, acc):
                window = fl[chunk, pl.ds(BLK + first - energy, BLK)]
                xr, xi, yr, yi, a, b, m1, m2 = products(window, energy, acc)
                return a + (xr * yi + xi * yr), b + (xr * yr - xi * yi), m1, m2

            a, b, m1, m2 = lax.fori_loop(0, first + BLK, step, blank, unroll=8)
            mixed = jnp.where(top_rows, -(m2 + pltpu.roll(m2, 4, 1)), pltpu.roll(m1, 4, 1) - m1)
            grid_out[first : first + BLK] = jnp.concatenate([-a, b, mixed], axis=1) * scale

        def to_slot(slot, carry):
            value = grid_out[slot_ref[slot]]
            out_ref[0, slot, :, cols] = jnp.concatenate([value[0:8], value[16:20]], axis=0).astype(BF16)
            out_ref[1, slot, :, cols] = jnp.concatenate([value[8:16], value[20:24]], axis=0).astype(BF16)
            return carry

        lax.fori_loop(0, ne, to_slot, 0, unroll=8)

    for chunk in range(chunks):
        sigma(chunk)

    for copy in copies:
        copy.wait_send()
    for chunk in range(chunks):
        sent(0, chunk, packed.at[chunk])
        sent(1, chunk, pout.at[chunk])
        sent(2, chunk, wout.at[chunk])


def shards(ne, nb, chunks, green, v_diag, v_low, energy_slot):
    size = v_diag.shape[-1]
    width = size // chunks
    rows = 24 * ne
    vmem = pl.BlockSpec(memory_space=pltpu.VMEM)
    hbm = pl.BlockSpec(memory_space=pltpu.HBM)
    scratch = (
        [pltpu.VMEM((ne, 48, width), BF16)] * chunks
        + [pltpu.VMEM((ne, 24, width), BF16)] * chunks
        + [pltpu.VMEM((ne, 24, width), BF16)] * chunks
        + [
            pltpu.VMEM((4, size, size), BF16),
            pltpu.VMEM((size, size), BF16),
            pltpu.VMEM((size, size), BF16),
            pltpu.SemaphoreType.DMA((3,)),
            pltpu.VMEM((chunks, ne, 48, width), BF16),
            pltpu.VMEM((chunks, ne, 24, width), BF16),
            pltpu.VMEM((chunks, ne, 24, width), BF16),
            pltpu.VMEM((chunks, rows, width), BF16),
            pltpu.VMEM((chunks, rows, width), BF16),
            pltpu.VMEM((chunks, rows, width), BF16),
            pltpu.VMEM((size, size), BF16),
            pltpu.VMEM((chunks, ne + 2 * BLK, 24, width), F32),
            pltpu.VMEM((ne, 32, width), F32),
            pltpu.VMEM((ne, 24, width), F32),
            pltpu.SMEM((ne,), jnp.int32),
            pltpu.VMEM((rows, size), BF16),
            pltpu.VMEM((rows, rows), BF16),
            pltpu.VMEM((rows, rows), BF16),
            pltpu.VMEM((rows, rows), BF16),
            pltpu.VMEM((size, size), BF16),
            pltpu.VMEM((size, size), BF16),
            pltpu.VMEM((rows, size), F32),
            pltpu.VMEM((rows, size), F32),
            pltpu.SemaphoreType.DMA((3 * chunks,)),
            pltpu.SemaphoreType.DMA((3 * chunks,)),
            pltpu.SemaphoreType.DMA((2 + 2 * chunks,)),
            pltpu.SemaphoreType.DMA((2 + 2 * chunks,)),
        ]
    )
    sigma = pl.pallas_call(
        functools.partial(kernel, ne, nb, chunks),
        out_shape=jax.ShapeDtypeStruct((2, ne, 12, size), BF16),
        in_specs=[pl.BlockSpec(memory_space=pltpu.SMEM), hbm, hbm, hbm],
        out_specs=vmem,
        scratch_shapes=scratch,
        compiler_params=pltpu.CompilerParams(
            collective_id=0, has_side_effects=True, vmem_limit_bytes=56 * 1024 * 1024
        ),
        cost_estimate=pl.CostEstimate(flops=2_500_000_000, bytes_accessed=4_000_000, transcendentals=0),
    )(energy_slot, green[:, 0, 0], v_diag[0], v_low[0])
    return sigma[:, :, None]


def solution(mesh):
    in_specs = (
        P(None, "energy", "space", None, None),
        P("space", None, None),
        P("space", None, None),
        P(),
    )
    out_specs = P(None, None, "space", "energy", None)
    body = functools.partial(shards, mesh.shape["energy"], mesh.shape["space"], 3)
    return jax.shard_map(body, mesh=mesh, in_specs=in_specs, out_specs=out_specs, check_vma=False)
```
